32 devices in a mesh: group: 2 (over y), lat: 4 (over z), chan: 2 (over x), lon: 2 (over core).
Axes of the slice: x: 2, y: 2, z: 4, core: 2. Of those that a mesh axis runs over, the one named last changes fastest.
Arguments:
- features: bfloat16 [32, 1440, 640], P('group', ('chan', 'lon'), 'lat'), parts along dimension 0, may hold values from -6 to 6
- basis: bfloat16 [16, 2, 5, 5], replicated, may hold values from -1.25 to 1.25
- block_start: int32 [16], replicated, may hold values from 0 to 4, as said below
- block_width: int32 [16], replicated, may hold values from 1 to 5, as said below
- weight: bfloat16 [1280, 640], P(None, ('chan', 'lon')), may hold values from -0.15625 to 0.15625
- cotangent: bfloat16 [32, 1440, 640], P(('group', 'lat'), ('chan', 'lon')), parts along dimension 0, may hold values from -6 to 6
Outputs:
- output: bfloat16 [32, 1440, 640], P(('group', 'lat'), ('chan', 'lon')), parts along dimension 0
- grad_input: bfloat16 [32, 1440, 640], P(('group', 'lat'), ('chan', 'lon')), parts along dimension 0
- grad_weight: float32 [2560, 640], P(('group', 'lat', 'chan', 'lon')), parts along dimension 0
The draws below stay inside these ranges and needn't reach their ends.
There are 2 independent parts, one for each index of `group`. The reference program is written for one: setup_inputs(seed, part) draws one part's arguments, and reference() takes and returns one part's arrays. A program takes and returns all parts, laid end to end along the dimension named above; an argument that names none is the same for every part. Nothing has to cross between parts.
Inputs may be any that keep to these rules, and one draw needn't show every extreme that they name: block_start + block_width <= 5 for every row; some row has block_start 5 - 1. Some row has block_width 5 and some row block_width 1.
All inputs are finite; a program needn't handle non-finite values.
Results may differ from the reference program's by a relative error of at most 0.005.
Values may be sent and summed in bfloat16 or wider, within the bound.
A program may use at most 128 MiB of HBM per device.

```python
import jax
import jax.numpy as jnp
from jax import lax

CH = 640
NLON = 1440
NBASIS = 2
REACH = 2
SPAN = 5
NLAT = 16


def block_pair(key):
    order = jax.random.permutation(jax.random.fold_in(key, 11), NLAT)
    widths = jax.random.randint(jax.random.fold_in(key, 12), (NLAT,), 1, SPAN + 1)
    widths = widths.at[order[0]].set(SPAN).at[order[1]].set(1)
    starts = jax.random.randint(jax.random.fold_in(key, 13), (NLAT,), 0, SPAN - widths + 1)
    starts = starts.at[order[1]].set(SPAN - 1).at[order[0]].set(0)
    return (starts.astype(jnp.int32), widths.astype(jnp.int32))


def draw_block_start(key, part):
    starts, widths = block_pair(key)
    return starts


def draw_block_width(key, part):
    starts, widths = block_pair(key)
    return widths


def levels(stream_key, extent, shards, low, largest):
    def one(axis_at, parts):
        steps = jax.random.uniform(jax.random.fold_in(jax.random.fold_in(stream_key, 6), axis_at), (parts,), jnp.float32, low / len(shards), largest / len(shards))
        return jnp.repeat(jnp.exp(steps), extent[axis_at] // parts).reshape((-1,) + (1,) * (len(extent) - axis_at - 1))

    level = one(*shards[0])
    for cut in shards[1:]:
        level = level * one(*cut)
    return level


def noise(rng, extent, spread, limit, pieces=(), held_as=jnp.bfloat16):
    entries = spread * jax.random.normal(rng, extent, jnp.float32)
    if pieces:
        entries = entries * levels(rng, extent, pieces, -0.22, 0.18)
    return jnp.clip(entries, -limit, limit).astype(held_as)


def setup_inputs(seed: int = 0, part: int = 0) -> dict:
    keys = jax.random.split(jax.random.key(seed), 7)
    own_keys = jax.random.split(jax.random.fold_in(keys[6], part), 7)
    features = noise(own_keys[0], (NLAT, NLON, CH), 1.0, 6.0, ((1, 4), (2, 4)))
    basis = noise(keys[1], (NLAT, NBASIS, SPAN, SPAN), (SPAN * SPAN) ** -0.5, 1.25)
    block_start = draw_block_start(jax.random.fold_in(keys[6], 71), part)
    block_width = draw_block_width(jax.random.fold_in(keys[6], 71), part)
    weight = noise(keys[4], (NBASIS * CH, CH), (NBASIS * CH) ** -0.5, 0.15625, ((1, 4),))
    cotangent = noise(own_keys[5], (NLAT, NLON, CH), 1.0, 6.0, ((0, 4), (1, 4)))
    return {"features": features, "basis": basis, "block_start": block_start, "block_width": block_width, "weight": weight, "cotangent": cotangent}


def masked_blocks(basis, block_start, block_width):
    column = jnp.arange(SPAN, dtype=jnp.int32)
    valid = (column[None, :] >= block_start[:, None]) & (column[None, :] < (block_start + block_width)[:, None])
    return jnp.where(valid[:, None, None, :], basis, jnp.zeros_like(basis))

def reference(features, basis, block_start, block_width, weight, cotangent):
    blocks = masked_blocks(basis, block_start, block_width).astype(jnp.float32)
    source = features.astype(jnp.float32)
    padded = jnp.pad(source, ((REACH, REACH), (0, 0), (0, 0)))
    total = jnp.zeros((NLAT, NLON, NBASIS, CH), jnp.float32)
    for offset_a in range(SPAN):
        window = padded[offset_a:offset_a + NLAT]
        for offset_b in range(SPAN):
            moved = jnp.roll(window, REACH - offset_b, axis=1)
            total = total + blocks[:, None, :, offset_a, offset_b, None] * moved[:, :, None, :]
    feats = total.reshape(NLAT * NLON, NBASIS * CH).astype(jnp.bfloat16)
    output = jnp.dot(feats, weight, preferred_element_type=jnp.float32).astype(jnp.bfloat16)
    output = output.reshape(NLAT, NLON, CH)
    flat_cot = cotangent.reshape(NLAT * NLON, CH)
    grad_feats = lax.dot_general(flat_cot, weight, (((1,), (1,)), ((), ())), preferred_element_type=jnp.float32)
    grad_feats = grad_feats.astype(jnp.bfloat16)
    grad_weight = lax.dot_general(feats, flat_cot, (((0,), (0,)), ((), ())), preferred_element_type=jnp.float32)
    grad_weight = grad_weight / jnp.sqrt(jnp.float32(NLAT * NLON))
    grads = grad_feats.astype(jnp.float32).reshape(NLAT, NLON, NBASIS, CH)
    grad_pad = jnp.pad(grads, ((REACH, REACH), (0, 0), (0, 0), (0, 0)))
    block_pad = jnp.pad(blocks, ((REACH, REACH), (0, 0), (0, 0), (0, 0)))
    result = jnp.zeros((NLAT, NLON, CH), jnp.float32)
    for offset_a in range(SPAN):
        begin = 2 * REACH - offset_a
        grad_rows = grad_pad[begin:begin + NLAT]
        block_rows = block_pad[begin:begin + NLAT]
        for offset_b in range(SPAN):
            moved = jnp.roll(grad_rows, offset_b - REACH, axis=1)
            result = result + jnp.einsum('jk,jnkc->jnc', block_rows[:, :, offset_a, offset_b], moved, precision=lax.Precision.HIGHEST)
    grad_input = result.astype(jnp.bfloat16)
    return (output, grad_input, grad_weight)
```

```python
import functools
import math

import jax
import jax.numpy as jnp
from jax import lax
from jax.experimental import pallas as pl
from jax.experimental.pallas import tpu as pltpu
from jax.sharding import PartitionSpec as P

REACH = 2


def padded(array, sides, width):
    for axis, dim in sides:
        size, length = (lax.axis_size(axis), array.shape[dim])
        up = [(i, (i + 1) % size) for i in range(size)]
        down = [(j, i) for i, j in up]
        last = lax.slice_in_dim(array, length - width, length, axis=dim)
        initial = lax.slice_in_dim(array, 0, width, axis=dim)
        before = lax.ppermute(last, axis, up)
        after = lax.ppermute(initial, axis, down)
        array = jnp.concatenate([before, array, after], axis=dim)
    return array


def extend(field, first, total_rows):
    haloed = padded(field, (("lat", 0), (("chan", "lon"), 1)), REACH)
    position = first - REACH + jnp.arange(haloed.shape[0], dtype=jnp.int32)
    inside = (position >= 0) & (position < total_rows)
    return jnp.where(inside[:, None, None], haloed, jnp.zeros_like(haloed))


def plain(features, basis, block_start, block_width, weight, cotangent):
    local = lax.all_to_all(features, "lat", split_axis=0, concat_axis=2, tiled=True)
    rows, width, chans = local.shape
    nbasis = basis.shape[1]
    span = 2 * REACH + 1
    total_rows = rows * lax.axis_size("lat")
    first = lax.axis_index("lat") * rows
    column = jnp.arange(span, dtype=jnp.int32)
    valid = (column[None, :] >= block_start[:, None]) & (
        column[None, :] < (block_start + block_width)[:, None]
    )
    blocks = jnp.where(valid[:, None, None, :], basis, jnp.zeros_like(basis))
    padded_blocks = jnp.pad(blocks, ((REACH, REACH), (0, 0), (0, 0), (0, 0)))
    near_blocks = lax.dynamic_slice_in_dim(padded_blocks, first, rows + 2 * REACH, 0).astype(
        jnp.float32
    )
    own_blocks = near_blocks[REACH : REACH + rows]
    reach_cols = width + 2 * REACH
    shift_table = (
        jnp.arange(reach_cols, dtype=jnp.int32)[None, :, None]
        - jnp.arange(width, dtype=jnp.int32)[:, None, None]
        == column[None, None, :]
    ).astype(jnp.float32)
    back_table = shift_table[:, :, ::-1]
    haloed = extend(local, first, total_rows)
    feat_parts = []
    for basis_k in range(nbasis):
        running = jnp.zeros((rows, width, chans), jnp.float32)
        for offset in range(span):
            row_map = jnp.einsum(
                "lmb,ib->ilm", shift_table, own_blocks[:, basis_k, offset, :]
            ).astype(jnp.bfloat16)
            running = running + jnp.einsum(
                "ilm,imc->ilc",
                row_map,
                haloed[offset : offset + rows],
                preferred_element_type=jnp.float32,
            )
        feat_parts.append(running.astype(jnp.bfloat16))
    feats = jnp.concatenate(feat_parts, axis=2)
    mixed = jnp.einsum(
        "ilj,jo->ilo",
        feats,
        lax.all_gather(weight, ("chan", "lon"), axis=1, tiled=True),
        preferred_element_type=jnp.float32,
    )
    grad_feats = jnp.einsum(
        "ilo,jo->ilj",
        cotangent,
        lax.all_gather(weight, ("chan", "lon"), axis=1, tiled=True),
        preferred_element_type=jnp.float32,
    )
    output = mixed.astype(jnp.bfloat16)
    factor = 1.0 / math.sqrt(total_rows * width * lax.axis_size(("chan", "lon")))
    grad_weight = lax.psum_scatter(
        lax.dot_general(
            feats, cotangent, (((0, 1), (0, 1)), ((), ())), preferred_element_type=jnp.float32
        )
        * factor,
        ("lat", "chan", "lon"),
        scatter_dimension=0,
        tiled=True,
    )
    grad_feats = grad_feats.astype(jnp.bfloat16)
    grad_halo = extend(grad_feats, first, total_rows)
    result = jnp.zeros((rows, width, chans), jnp.float32)
    for offset in range(span):
        begin = 2 * REACH - offset
        source_rows = grad_halo[begin : begin + rows]
        block_rows = near_blocks[begin : begin + rows]
        for basis_k in range(nbasis):
            back_map = jnp.einsum(
                "nmb,jb->jnm", back_table, block_rows[:, basis_k, offset, :]
            ).astype(jnp.bfloat16)
            source_part = source_rows[:, :, basis_k * chans : (basis_k + 1) * chans]
            result = result + jnp.einsum(
                "jnm,jmc->jnc", back_map, source_part, preferred_element_type=jnp.float32
            )
    grad_input = result.astype(jnp.bfloat16)
    return (output, grad_input, grad_weight)


SPAN = 2 * REACH + 1
TILE = 128
WINDOW = TILE + 16
MESH = pl.DeviceIdType.MESH


def ring_edges(array):
    axes = ("chan", "lon")
    size, width = lax.axis_size(axes), array.shape[1]
    up = [(i, (i + 1) % size) for i in range(size)]
    before = lax.ppermute(array[:, width - REACH :], axes, up)
    after = lax.ppermute(array[:, :REACH], axes, [(j, i) for i, j in up])
    fill = -(width + 2 * REACH) % 16
    zeros = jnp.zeros((array.shape[0], fill, array.shape[2]), array.dtype)
    return jnp.concatenate([before, array, after, zeros], axis=1)


def band_maps(basis, block_start, block_width, rows):
    column = jnp.arange(SPAN, dtype=jnp.int32)
    valid = (column[None, :] >= block_start[:, None]) & (
        column[None, :] < (block_start + block_width)[:, None]
    )
    blocks = jnp.where(valid[:, None, None, :], basis, jnp.zeros_like(basis))
    blocks = jnp.pad(blocks, ((REACH, REACH), (0, 0), (0, 0), (0, 0)))
    first = lax.axis_index("lat") * rows
    near = lax.dynamic_slice_in_dim(blocks, first, rows + 2 * REACH, 0)
    own = near[REACH : REACH + rows]
    nbasis = basis.shape[1]
    shift = jnp.arange(WINDOW, dtype=jnp.int32)[None, :] - jnp.arange(TILE, dtype=jnp.int32)[:, None]
    forward = jnp.zeros((rows, nbasis, TILE, SPAN, WINDOW), basis.dtype)
    for b in range(SPAN):
        hit = (shift == b)[None, None, :, None, :]
        forward = jnp.where(hit, own[:, :, :, b][:, :, None, :, None], forward)
    source = jnp.stack(
        [jnp.stack([near[i + q, :, SPAN - 1 - q, :] for q in range(SPAN)]) for i in range(rows)]
    )
    backward = jnp.zeros((rows, TILE, SPAN, nbasis, WINDOW), basis.dtype)
    for b in range(SPAN):
        hit = (shift == SPAN - 1 - b)[None, :, None, None, :]
        backward = jnp.where(hit, source[:, None, :, :, b, None], backward)
    return (
        forward.reshape(rows, nbasis * TILE, SPAN * WINDOW),
        backward.reshape(rows, TILE, SPAN * nbasis * WINDOW),
    )


def layer_kernel(
    nlat, nchan, nlon, factor,
    field, cot_ext, weight_t, cot, forward, backward,
    out, grad_in, grad_w,
    landed, near, cots, mixing, gathered, feats, grads, total,
    send1, recv1, send2, recv2, send3, recv3,
    f_send, f_recv, fwd_send, w_send, w_recv, c_send, c_recv, own_sem, g_send, g_recv,
):
    z, x, core = lax.axis_index("lat"), lax.axis_index("chan"), lax.axis_index("lon")
    rows, width, chs = cot.shape
    ext, part = field.shape[1], field.shape[2]
    wide = near.shape[1]
    tiles = (width + TILE - 1) // TILE
    nshard = nchan * nlon
    mine = x * nlon + core
    block = grad_w.shape[0]
    last = rows + REACH

    barrier = pltpu.get_barrier_semaphore()
    for t in range(nlat):
        @pl.when(z != t)
        def _():
            pl.semaphore_signal(barrier, inc=1, device_id={"lat": t}, device_id_type=MESH)
    for s in range(nshard):
        @pl.when(mine != s)
        def _():
            pl.semaphore_signal(
                barrier, inc=1, device_id={"chan": s // nlon, "lon": s % nlon}, device_id_type=MESH
            )
    pl.semaphore_wait(barrier, nlat - 1 + nshard - 1)

    def piece(t, kind):
        if kind == 0:
            return rows * t, REACH, rows
        if kind == 1:
            return rows * t - REACH, 0, REACH
        return rows * (t + 1), last, REACH

    def field_copy(t, kind):
        begin, at, count = piece(t, kind)
        return pltpu.make_async_remote_copy(
            src_ref=field.at[pl.ds(begin, count)],
            dst_ref=landed.at[z, pl.ds(at, count)],
            send_sem=f_send.at[t, kind],
            recv_sem=f_recv.at[z, kind],
            device_id={"lat": t},
            device_id_type=MESH,
        )

    def arrival(j, kind):
        _, at, count = piece(1, kind)
        return pltpu.make_async_remote_copy(
            src_ref=field.at[pl.ds(0, count)],
            dst_ref=landed.at[j, pl.ds(at, count)],
            send_sem=f_send.at[0, kind],
            recv_sem=f_recv.at[j, kind],
            device_id={"lat": 0},
            device_id_type=MESH,
        )

    def direct(t, kind):
        if kind == 0:
            return z != t
        if kind == 1:
            return ((z > t) | (z == t - 1)) if t > 0 else None
        return ((z < t) | (z == t + 1)) if t < nlat - 1 else None

    kinds = ((t, kind) for kind in (0, 1, 2) for t in range(nlat))
    sends = [(t, kind, direct(t, kind)) for t, kind in kinds if direct(t, kind) is not None]
    for t, kind, when in sends:
        @pl.when(when)
        def _():
            field_copy(t, kind).start()

    def own_copy(t, kind):
        begin, at, count = piece(t, kind)
        return pltpu.make_async_copy(
            field.at[pl.ds(begin, count)], landed.at[t, pl.ds(at, count)], own_sem.at[kind]
        )

    for t, kind, _when in sends:
        @pl.when(z == t)
        def _():
            own_copy(t, kind).start()

    def weight_copy(s):
        return pltpu.make_async_remote_copy(
            src_ref=weight_t,
            dst_ref=gathered.at[mine],
            send_sem=w_send.at[s],
            recv_sem=w_recv.at[mine],
            device_id={"chan": s // nlon, "lon": s % nlon},
            device_id_type=MESH,
        )

    for s in range(nshard):
        @pl.when(mine != s)
        def _():
            weight_copy(s).start()
    own_weight = pltpu.make_async_copy(weight_t, gathered.at[mine], own_sem.at[3])
    own_weight.start()
    own_cot = pltpu.make_async_copy(cot_ext, cots.at[pl.ds(REACH, rows)], own_sem.at[4])
    own_cot.start()

    def cot_copy(way):
        begin, at = ((rows - REACH, 0), (0, last))[way]
        return pltpu.make_async_remote_copy(
            src_ref=cot_ext.at[pl.ds(begin, REACH)],
            dst_ref=cots.at[pl.ds(at, REACH)],
            send_sem=c_send.at[way],
            recv_sem=c_recv.at[way],
            device_id={"lat": z + 1 - 2 * way},
            device_id_type=MESH,
        )

    has_up, has_down = z < nlat - 1, z > 0

    @pl.when(has_up)
    def _():
        cot_copy(0).start()

    @pl.when(has_down)
    def _():
        cot_copy(1).start()

    if wide > ext:
        near[:, pl.ds(ext, wide - ext), :] = jnp.zeros((rows + 2 * REACH, wide - ext, chs), near.dtype)
        grads[:, pl.ds(ext, wide - ext), :] = jnp.zeros(
            (rows + 2 * REACH, wide - ext, grads.shape[2]), grads.dtype
        )

    @pl.when(jnp.logical_not(has_down))
    def _():
        cots[pl.ds(0, REACH)] = jnp.zeros((REACH, ext, chs), cots.dtype)
        landed[:, pl.ds(0, REACH)] = jnp.zeros((nlat, REACH, ext, part), landed.dtype)

    @pl.when(jnp.logical_not(has_up))
    def _():
        cots[pl.ds(last, REACH)] = jnp.zeros((REACH, ext, chs), cots.dtype)
        landed[:, pl.ds(last, REACH)] = jnp.zeros((nlat, REACH, ext, part), landed.dtype)

    own_weight.wait()
    for s in range(nshard):
        @pl.when(mine != s)
        def _():
            pltpu.make_async_remote_copy(
                src_ref=weight_t, dst_ref=gathered.at[s], send_sem=w_send.at[s],
                recv_sem=w_recv.at[s], device_id={"chan": s // nlon, "lon": s % nlon},
                device_id_type=MESH,
            ).wait_recv()
    mixing[...] = gathered[...].reshape(mixing.shape)

    def feature_gradient(q):
        grads[q, pl.ds(0, ext), :] = jnp.dot(
            cots[q], mixing[...], preferred_element_type=jnp.float32
        ).astype(grads.dtype)

    own_cot.wait()

    @pl.loop(REACH, last)
    def _(q):
        feature_gradient(q)

    def pass_on(j, way):
        begin, at, kind = ((last - REACH, 0, 1), (REACH, last, 2))[way]
        return pltpu.make_async_remote_copy(
            src_ref=landed.at[j, pl.ds(begin, REACH)],
            dst_ref=landed.at[j, pl.ds(at, REACH)],
            send_sem=fwd_send.at[j, way],
            recv_sem=f_recv.at[j, kind],
            device_id={"lat": z + 1 - 2 * way},
            device_id_type=MESH,
        )

    for t, kind, _when in sends:
        @pl.when(z == t)
        def _():
            own_copy(t, kind).wait()
    for j in range(nlat):
        @pl.when(z != j)
        def _():
            arrival(j, 0).wait_recv()
        @pl.when(has_up & (j < z))
        def _():
            pass_on(j, 0).start()
        @pl.when(has_down & (j > z))
        def _():
            pass_on(j, 1).start()
    for j in range(nlat):
        @pl.when((z != j) & has_down)
        def _():
            arrival(j, 1).wait_recv()
        @pl.when((z != j) & has_up)
        def _():
            arrival(j, 2).wait_recv()

    @pl.loop(0, rows + 2 * REACH)
    def _(q):
        near[q, pl.ds(0, ext), :] = jnp.concatenate([landed[j, q] for j in range(nlat)], axis=-1)

    nbasis = forward.shape[1] // TILE
    total[...] = jnp.zeros_like(total)

    @pl.loop(0, rows)
    def _(i):
        for tile in range(tiles):
            source = jnp.concatenate(
                [near[i + a, pl.ds(tile * TILE, WINDOW), :] for a in range(SPAN)], axis=0
            )
            made = jnp.dot(forward[i], source, preferred_element_type=jnp.float32)
            for k in range(nbasis):
                feats[i, pl.ds(tile * TILE, TILE), pl.ds(k * chs, chs)] = made[
                    k * TILE : (k + 1) * TILE
                ].astype(feats.dtype)
        held = feats[i, pl.ds(0, width), :]
        total[...] += lax.dot_general(
            held, cot[i], (((0,), (0,)), ((), ())), preferred_element_type=jnp.float32
        )

    def term(l, c, o):
        at = ((l * nchan + c) * nlon + o) * block
        return total[pl.ds(pl.multiple_of(at, 16), block), :]

    def exchange(send, recv, n, device):
        return pltpu.make_async_remote_copy(
            src_ref=send, dst_ref=recv, send_sem=g_send.at[n], recv_sem=g_recv.at[n],
            device_id=device, device_id_type=MESH,
        )

    for l in range(nlat):
        for c in range(nchan):
            send1[l, c] = term(l, c, 1 - core).astype(send1.dtype)
    over_core = exchange(send1, recv1, 0, {"lon": 1 - core})
    over_core.start()

    @pl.loop(0, rows)
    def _(i):
        out[i] = lax.dot_general(
            feats[i, pl.ds(0, width), :], mixing[...], (((1,), (1,)), ((), ())),
            preferred_element_type=jnp.float32,
        ).astype(out.dtype)

    over_core.wait()

    for l in range(nlat):
        value = term(l, 1 - x, core) + recv1[l, 1 - x].astype(jnp.float32)
        send2[l] = value.astype(send2.dtype)
    over_x = exchange(send2, recv2, 1, {"chan": 1 - x})
    over_x.start()

    @pl.when(has_down)
    def _():
        cot_copy(0).wait_recv()

    @pl.when(has_up)
    def _():
        cot_copy(1).wait_recv()

    for q in (0, 1, last, last + 1):
        feature_gradient(q)
    over_x.wait()

    def over_z(t):
        return pltpu.make_async_remote_copy(
            src_ref=send3.at[t], dst_ref=recv3.at[z], send_sem=g_send.at[2 + t],
            recv_sem=g_recv.at[2 + z], device_id={"lat": t}, device_id_type=MESH,
        )

    def reduced(t):
        return term(t, x, core) + recv1[t, x].astype(jnp.float32) + recv2[t].astype(jnp.float32)

    for t in range(nlat):
        @pl.when(z != t)
        def _():
            send3[t] = reduced(t).astype(send3.dtype)
            over_z(t).start()

    @pl.loop(0, rows)
    def _(i):
        for tile in range(tiles):
            source = jnp.concatenate(
                [
                    grads[i + q, pl.ds(tile * TILE, WINDOW), pl.ds(k * chs, chs)]
                    for q in range(SPAN)
                    for k in range(nbasis)
                ],
                axis=0,
            )
            made = jnp.dot(backward[i], source, preferred_element_type=jnp.float32)
            count = min(TILE, width - tile * TILE)
            grad_in[i, pl.ds(tile * TILE, count), :] = made[:count].astype(grad_in.dtype)

    grad_w[...] = reduced(z)
    for j in range(nlat):
        @pl.when(z != j)
        def _():
            pltpu.make_async_remote_copy(
                src_ref=send3.at[j], dst_ref=recv3.at[j], send_sem=g_send.at[2 + j],
                recv_sem=g_recv.at[2 + j], device_id={"lat": j}, device_id_type=MESH,
            ).wait_recv()
            grad_w[...] += recv3[j].astype(jnp.float32)
    grad_w[...] = grad_w[...] * factor

    for t in range(nlat):
        @pl.when(z != t)
        def _():
            over_z(t).wait_send()
    for t, kind, when in sends:
        @pl.when(when)
        def _():
            field_copy(t, kind).wait_send()
    for s in range(nshard):
        @pl.when(mine != s)
        def _():
            weight_copy(s).wait_send()
    for j in range(nlat):
        @pl.when(has_up & (j < z))
        def _():
            pass_on(j, 0).wait_send()
        @pl.when(has_down & (j > z))
        def _():
            pass_on(j, 1).wait_send()

    @pl.when(has_up)
    def _():
        cot_copy(0).wait_send()

    @pl.when(has_down)
    def _():
        cot_copy(1).wait_send()


def fused(features, basis, block_start, block_width, weight, cotangent):
    nlat, nchan, nlon = (lax.axis_size(a) for a in ("lat", "chan", "lon"))
    rows, width, chs = cotangent.shape
    part, depth = features.shape[2], weight.shape[0]
    factor = 1.0 / math.sqrt(rows * nlat * width * nchan * nlon)
    forward, backward = band_maps(basis, block_start, block_width, rows)
    field, cot_ext = ring_edges(features), ring_edges(cotangent)
    ext = field.shape[1]
    tiles = (width + TILE - 1) // TILE
    wide = max(ext, (tiles - 1) * TILE + WINDOW)
    tall, block = rows + 2 * REACH, depth // (nlat * nchan * nlon)
    half = jnp.bfloat16
    dma = pltpu.SemaphoreType.DMA
    vmem, anywhere = pl.BlockSpec(memory_space=pltpu.VMEM), pl.BlockSpec(memory_space=pl.ANY)
    return pl.pallas_call(
        functools.partial(layer_kernel, nlat, nchan, nlon, factor),
        out_shape=(
            jax.ShapeDtypeStruct((rows, width, chs), half),
            jax.ShapeDtypeStruct((rows, width, chs), half),
            jax.ShapeDtypeStruct((block, chs), jnp.float32),
        ),
        in_specs=[anywhere, anywhere, anywhere, vmem, vmem, vmem],
        out_specs=(vmem, vmem, vmem),
        scratch_shapes=[
            pltpu.VMEM((nlat, tall, ext, part), half),
            pltpu.VMEM((tall, wide, chs), half),
            pltpu.VMEM((tall, ext, chs), half),
            pltpu.VMEM((chs, depth), half),
            pltpu.VMEM((nchan * nlon, chs // (nchan * nlon), depth), half),
            pltpu.VMEM((rows, tiles * TILE, depth), half),
            pltpu.VMEM((tall, wide, depth), half),
            pltpu.VMEM((depth, chs), jnp.float32),
            pltpu.VMEM((nlat, nchan, block, chs), half),
            pltpu.VMEM((nlat, nchan, block, chs), half),
            pltpu.VMEM((nlat, block, chs), half),
            pltpu.VMEM((nlat, block, chs), half),
            pltpu.VMEM((nlat, block, chs), half),
            pltpu.VMEM((nlat, block, chs), half),
            dma((nlat, 3)),
            dma((nlat, 3)),
            dma((nlat, 2)),
            dma((nchan * nlon,)),
            dma((nchan * nlon,)),
            dma((2,)),
            dma((2,)),
            dma((5,)),
            dma((2 + nlat,)),
            dma((2 + nlat,)),
        ],
        compiler_params=pltpu.CompilerParams(
            collective_id=0, has_side_effects=True, vmem_limit_bytes=60 * 1024 * 1024
        ),
    )(field, cot_ext, weight.T, cotangent, forward, backward)


def on_device(features, basis, block_start, block_width, weight, cotangent):
    nlat, nchan, nlon = (lax.axis_size(a) for a in ("lat", "chan", "lon"))
    rows, _, chs = cotangent.shape
    shards = nchan * nlon
    tiled = chs % 128 == 0 and (chs // shards) % 16 == 0 and (weight.shape[0] // (nlat * shards)) % 16 == 0
    if tiled and nchan == 2 and nlon == 2 and nlat > 1 and rows >= REACH:
        run = fused
    else:
        run = plain
    return run(features, basis, block_start, block_width, weight, cotangent)


def solution(mesh):
    return jax.shard_map(
        on_device,
        mesh=mesh,
        in_specs=(
            P("group", ("chan", "lon"), "lat"),
            P(),
            P(),
            P(),
            P(None, ("chan", "lon")),
            P(("group", "lat"), ("chan", "lon"), None),
        ),
        out_specs=(
            P(("group", "lat"), ("chan", "lon"), None),
            P(("group", "lat"), ("chan", "lon"), None),
            P(("group", "lat", "chan", "lon"), None),
        ),
        check_vma=False,
    )
```

```python
import functools
import math

import jax
import jax.numpy as jnp
from jax import lax
from jax.experimental import pallas as pl
from jax.experimental.pallas import tpu as pltpu
from jax.sharding import PartitionSpec as P

REACH = 2


def padded(array, sides, width):
    for axis, dim in sides:
        size, length = (lax.axis_size(axis), array.shape[dim])
        up = [(i, (i + 1) % size) for i in range(size)]
        down = [(j, i) for i, j in up]
        last = lax.slice_in_dim(array, length - width, length, axis=dim)
        initial = lax.slice_in_dim(array, 0, width, axis=dim)
        before = lax.ppermute(last, axis, up)
        after = lax.ppermute(initial, axis, down)
        array = jnp.concatenate([before, array, after], axis=dim)
    return array


def extend(field, first, total_rows):
    haloed = padded(field, (("lat", 0), (("chan", "lon"), 1)), REACH)
    position = first - REACH + jnp.arange(haloed.shape[0], dtype=jnp.int32)
    inside = (position >= 0) & (position < total_rows)
    return jnp.where(inside[:, None, None], haloed, jnp.zeros_like(haloed))


def plain(features, basis, block_start, block_width, weight, cotangent):
    local = lax.all_to_all(features, "lat", split_axis=0, concat_axis=2, tiled=True)
    rows, width, chans = local.shape
    nbasis = basis.shape[1]
    span = 2 * REACH + 1
    total_rows = rows * lax.axis_size("lat")
    first = lax.axis_index("lat") * rows
    column = jnp.arange(span, dtype=jnp.int32)
    valid = (column[None, :] >= block_start[:, None]) & (
        column[None, :] < (block_start + block_width)[:, None]
    )
    blocks = jnp.where(valid[:, None, None, :], basis, jnp.zeros_like(basis))
    padded_blocks = jnp.pad(blocks, ((REACH, REACH), (0, 0), (0, 0), (0, 0)))
    near_blocks = lax.dynamic_slice_in_dim(padded_blocks, first, rows + 2 * REACH, 0).astype(
        jnp.float32
    )
    own_blocks = near_blocks[REACH : REACH + rows]
    reach_cols = width + 2 * REACH
    shift_table = (
        jnp.arange(reach_cols, dtype=jnp.int32)[None, :, None]
        - jnp.arange(width, dtype=jnp.int32)[:, None, None]
        == column[None, None, :]
    ).astype(jnp.float32)
    back_table = shift_table[:, :, ::-1]
    haloed = extend(local, first, total_rows)
    feat_parts = []
    for basis_k in range(nbasis):
        running = jnp.zeros((rows, width, chans), jnp.float32)
        for offset in range(span):
            row_map = jnp.einsum(
                "lmb,ib->ilm", shift_table, own_blocks[:, basis_k, offset, :]
            ).astype(jnp.bfloat16)
            running = running + jnp.einsum(
                "ilm,imc->ilc",
                row_map,
                haloed[offset : offset + rows],
                preferred_element_type=jnp.float32,
            )
        feat_parts.append(running.astype(jnp.bfloat16))
    feats = jnp.concatenate(feat_parts, axis=2)
    mixed = jnp.einsum(
        "ilj,jo->ilo",
        feats,
        lax.all_gather(weight, ("chan", "lon"), axis=1, tiled=True),
        preferred_element_type=jnp.float32,
    )
    grad_feats = jnp.einsum(
        "ilo,jo->ilj",
        cotangent,
        lax.all_gather(weight, ("chan", "lon"), axis=1, tiled=True),
        preferred_element_type=jnp.float32,
    )
    output = mixed.astype(jnp.bfloat16)
    factor = 1.0 / math.sqrt(total_rows * width * lax.axis_size(("chan", "lon")))
    grad_weight = lax.psum_scatter(
        lax.dot_general(
            feats, cotangent, (((0, 1), (0, 1)), ((), ())), preferred_element_type=jnp.float32
        )
        * factor,
        ("lat", "chan", "lon"),
        scatter_dimension=0,
        tiled=True,
    )
    grad_feats = grad_feats.astype(jnp.bfloat16)
    grad_halo = extend(grad_feats, first, total_rows)
    result = jnp.zeros((rows, width, chans), jnp.float32)
    for offset in range(span):
        begin = 2 * REACH - offset
        source_rows = grad_halo[begin : begin + rows]
        block_rows = near_blocks[begin : begin + rows]
        for basis_k in range(nbasis):
            back_map = jnp.einsum(
                "nmb,jb->jnm", back_table, block_rows[:, basis_k, offset, :]
            ).astype(jnp.bfloat16)
            source_part = source_rows[:, :, basis_k * chans : (basis_k + 1) * chans]
            result = result + jnp.einsum(
                "jnm,jmc->jnc", back_map, source_part, preferred_element_type=jnp.float32
            )
    grad_input = result.astype(jnp.bfloat16)
    return (output, grad_input, grad_weight)


SPAN = 2 * REACH + 1
TILE = 128
WINDOW = TILE + 16
MESH = pl.DeviceIdType.MESH


def ring_edges(array, dim, multiple):
    axes = ("chan", "lon")
    size, width = lax.axis_size(axes), array.shape[dim]
    up = [(i, (i + 1) % size) for i in range(size)]
    final = lax.slice_in_dim(array, width - REACH, width, axis=dim)
    initial = lax.slice_in_dim(array, 0, REACH, axis=dim)
    before = lax.ppermute(final, axes, up)
    after = lax.ppermute(initial, axes, [(j, i) for i, j in up])
    shape = list(array.shape)
    shape[dim] = -(width + 2 * REACH) % multiple
    return jnp.concatenate([before, array, after, jnp.zeros(shape, array.dtype)], axis=dim)


def layer_kernel(
    nlat, nchan, nlon, factor,
    field, cot_ext, weight_t, cot, basis, start, count_used,
    out, grad_in, grad_w,
    forward, backward, landed, cots, mixing, gathered, feats, grads, total,
    send1, recv1, send2, recv2, send3, recv3,
    f_send, f_recv, fwd_send, w_send, w_recv, c_send, c_recv, own_sem, g_send, g_recv,
):
    z, x, core = lax.axis_index("lat"), lax.axis_index("chan"), lax.axis_index("lon")
    rows, width, chs = cot.shape
    ext, part, lanes = cot_ext.shape[1], field.shape[1], field.shape[2]
    wide = grads.shape[1]
    tiles = (width + TILE - 1) // TILE
    nshard = nchan * nlon
    mine = x * nlon + core
    block = grad_w.shape[0]
    last = rows + REACH

    barrier = pltpu.get_barrier_semaphore()
    for t in range(nlat):
        @pl.when(z != t)
        def _():
            pl.semaphore_signal(barrier, inc=1, device_id={"lat": t}, device_id_type=MESH)
    for s in range(nshard):
        @pl.when(mine != s)
        def _():
            pl.semaphore_signal(
                barrier, inc=1, device_id={"chan": s // nlon, "lon": s % nlon}, device_id_type=MESH
            )
    pl.semaphore_wait(barrier, nlat - 1 + nshard - 1)

    def channels(j):
        return pl.ds(pl.multiple_of(j * part, 16), part)

    def piece(t, kind):
        if kind == 0:
            return rows * t, REACH, rows
        if kind == 1:
            return rows * t - REACH, 0, REACH
        return rows * (t + 1), last, REACH

    def field_copy(t, kind):
        begin, at, count = piece(t, kind)
        return pltpu.make_async_remote_copy(
            src_ref=field.at[pl.ds(begin, count)],
            dst_ref=landed.at[pl.ds(at, count), channels(z), :],
            send_sem=f_send.at[t, kind],
            recv_sem=f_recv.at[z, kind],
            device_id={"lat": t},
            device_id_type=MESH,
        )

    def arrival(j, kind):
        _, at, count = piece(1, kind)
        return pltpu.make_async_remote_copy(
            src_ref=field.at[pl.ds(0, count)],
            dst_ref=landed.at[pl.ds(at, count), channels(j), :],
            send_sem=f_send.at[0, kind],
            recv_sem=f_recv.at[j, kind],
            device_id={"lat": 0},
            device_id_type=MESH,
        )

    def direct(t, kind):
        if kind == 0:
            return z != t
        if kind == 1:
            return ((z > t) | (z == t - 1)) if t > 0 else None
        return ((z < t) | (z == t + 1)) if t < nlat - 1 else None

    kinds = ((t, kind) for kind in (0, 1, 2) for t in range(nlat))
    sends = [(t, kind, direct(t, kind)) for t, kind in kinds if direct(t, kind) is not None]
    for t, kind, when in sends:
        @pl.when(when)
        def _():
            field_copy(t, kind).start()

    def own_copy(t, kind):
        begin, at, count = piece(t, kind)
        return pltpu.make_async_copy(
            field.at[pl.ds(begin, count)], landed.at[pl.ds(at, count), channels(t), :], own_sem.at[kind]
        )

    for t, kind, _when in sends:
        @pl.when(z == t)
        def _():
            own_copy(t, kind).start()

    def weight_copy(s):
        return pltpu.make_async_remote_copy(
            src_ref=weight_t,
            dst_ref=gathered.at[mine],
            send_sem=w_send.at[s],
            recv_sem=w_recv.at[mine],
            device_id={"chan": s // nlon, "lon": s % nlon},
            device_id_type=MESH,
        )

    for s in range(nshard):
        @pl.when(mine != s)
        def _():
            weight_copy(s).start()
    own_weight = pltpu.make_async_copy(weight_t, gathered.at[mine], own_sem.at[3])
    own_weight.start()
    own_cot = pltpu.make_async_copy(cot_ext, cots.at[pl.ds(REACH, rows)], own_sem.at[4])
    own_cot.start()

    def cot_copy(way):
        begin, at = ((rows - REACH, 0), (0, last))[way]
        return pltpu.make_async_remote_copy(
            src_ref=cot_ext.at[pl.ds(begin, REACH)],
            dst_ref=cots.at[pl.ds(at, REACH)],
            send_sem=c_send.at[way],
            recv_sem=c_recv.at[way],
            device_id={"lat": z + 1 - 2 * way},
            device_id_type=MESH,
        )

    has_up, has_down = z < nlat - 1, z > 0

    if wide > ext:
        grads[:, pl.ds(ext, wide - ext), :] = jnp.zeros(
            (rows + 2 * REACH, wide - ext, grads.shape[2]), grads.dtype
        )

    @pl.when(jnp.logical_not(has_down))
    def _():
        cots[pl.ds(0, REACH)] = jnp.zeros((REACH, ext, chs), cots.dtype)
        landed[pl.ds(0, REACH)] = jnp.zeros((REACH, chs, lanes), landed.dtype)

    @pl.when(jnp.logical_not(has_up))
    def _():
        cots[pl.ds(last, REACH)] = jnp.zeros((REACH, ext, chs), cots.dtype)
        landed[pl.ds(last, REACH)] = jnp.zeros((REACH, chs, lanes), landed.dtype)

    shift = lax.broadcasted_iota(jnp.int32, (TILE, WINDOW), 1) - lax.broadcasted_iota(
        jnp.int32, (TILE, WINDOW), 0
    )
    total_rows = rows * nlat
    nbasis = basis.shape[1] // (SPAN * SPAN)

    def value(row, k, a, b):
        held = jnp.clip(row, 0, total_rows - 1)
        used = (b >= start[held]) & (b < start[held] + count_used[held])
        used = used & (row >= 0) & (row < total_rows)
        return jnp.where(used, basis[held, (k * SPAN + a) * SPAN + b], 0.0)

    turned = lax.broadcasted_iota(jnp.int32, (2 * TILE, TILE), 0) - lax.broadcasted_iota(
        jnp.int32, (2 * TILE, TILE), 1
    )

    def band(row, k, a, back):
        offset = shift if back else turned
        made = jnp.zeros(offset.shape, jnp.float32)
        for b in range(SPAN):
            made = jnp.where(offset == (SPAN - 1 - b if back else b), value(row, k, a, b), made)
        return made

    @pl.loop(0, rows)
    def _(i):
        row = z * rows + i
        for k in range(nbasis):
            for a in range(SPAN):
                forward[i, a, :, pl.ds(k * TILE, TILE)] = band(row, k, a, False).astype(forward.dtype)
        backward[i] = jnp.concatenate(
            [
                band(row + q - REACH, k, SPAN - 1 - q, True)
                for q in range(SPAN)
                for k in range(nbasis)
            ],
            axis=1,
        ).astype(backward.dtype)

    own_weight.wait()
    for s in range(nshard):
        @pl.when(mine != s)
        def _():
            pltpu.make_async_remote_copy(
                src_ref=weight_t, dst_ref=gathered.at[s], send_sem=w_send.at[s],
                recv_sem=w_recv.at[s], device_id={"chan": s // nlon, "lon": s % nlon},
                device_id_type=MESH,
            ).wait_recv()
    mixing[...] = gathered[...].reshape(mixing.shape)

    def feature_gradient(q):
        grads[q, pl.ds(0, ext), :] = jnp.dot(
            cots[q], mixing[...], preferred_element_type=jnp.float32
        ).astype(grads.dtype)

    own_cot.wait()

    @pl.loop(REACH, last)
    def _(q):
        feature_gradient(q)

    def pass_on(j, way):
        begin, at, kind = ((last - REACH, 0, 1), (REACH, last, 2))[way]
        return pltpu.make_async_remote_copy(
            src_ref=landed.at[pl.ds(begin, REACH), channels(j), :],
            dst_ref=landed.at[pl.ds(at, REACH), channels(j), :],
            send_sem=fwd_send.at[j, way],
            recv_sem=f_recv.at[j, kind],
            device_id={"lat": z + 1 - 2 * way},
            device_id_type=MESH,
        )

    for t, kind, _when in sends:
        @pl.when(z == t)
        def _():
            own_copy(t, kind).wait()
    for j in range(nlat):
        @pl.when(z != j)
        def _():
            arrival(j, 0).wait_recv()
        @pl.when(has_up & (j < z))
        def _():
            pass_on(j, 0).start()
        @pl.when(has_down & (j > z))
        def _():
            pass_on(j, 1).start()
    for j in range(nlat):
        @pl.when((z != j) & has_down)
        def _():
            arrival(j, 1).wait_recv()
        @pl.when((z != j) & has_up)
        def _():
            arrival(j, 2).wait_recv()

    @pl.when(has_up)
    def _():
        cot_copy(0).start()

    @pl.when(has_down)
    def _():
        cot_copy(1).start()

    total[...] = jnp.zeros_like(total)

    @pl.loop(0, rows)
    def _(i):
        for tile in range(tiles):
            reach = min(2 * TILE, lanes - tile * TILE)
            made = jnp.zeros((chs, nbasis * TILE), jnp.float32)
            for a in range(SPAN):
                made = made + jnp.dot(
                    landed[i + a, :, pl.ds(tile * TILE, reach)],
                    forward[i, a, pl.ds(0, reach), :],
                    preferred_element_type=jnp.float32,
                )
            for k in range(nbasis):
                feats[i, pl.ds(k * chs, chs), pl.ds(tile * TILE, TILE)] = made[
                    :, k * TILE : (k + 1) * TILE
                ].astype(feats.dtype)
        total[...] += jnp.dot(
            feats[i, :, pl.ds(0, width)], cot[i], preferred_element_type=jnp.float32
        )

    def term(l, c, o):
        at = ((l * nchan + c) * nlon + o) * block
        return total[pl.ds(pl.multiple_of(at, 16), block), :]

    def exchange(send, recv, n, device):
        return pltpu.make_async_remote_copy(
            src_ref=send, dst_ref=recv, send_sem=g_send.at[n], recv_sem=g_recv.at[n],
            device_id=device, device_id_type=MESH,
        )

    for l in range(nlat):
        for c in range(nchan):
            send1[l, c] = term(l, c, 1 - core).astype(send1.dtype)
    over_core = exchange(send1, recv1, 0, {"lon": 1 - core})
    over_core.start()

    @pl.loop(0, rows)
    def _(i):
        mixed = jnp.dot(mixing[...], feats[i], preferred_element_type=jnp.float32)
        out[i] = mixed.T[:width].astype(out.dtype)

    over_core.wait()

    for l in range(nlat):
        value = term(l, 1 - x, core) + recv1[l, 1 - x].astype(jnp.float32)
        send2[l] = value.astype(send2.dtype)
    over_x = exchange(send2, recv2, 1, {"chan": 1 - x})
    over_x.start()

    @pl.when(has_down)
    def _():
        cot_copy(0).wait_recv()

    @pl.when(has_up)
    def _():
        cot_copy(1).wait_recv()

    for q in (0, 1, last, last + 1):
        feature_gradient(q)
    over_x.wait()

    def over_z(t):
        return pltpu.make_async_remote_copy(
            src_ref=send3.at[t], dst_ref=recv3.at[z], send_sem=g_send.at[2 + t],
            recv_sem=g_recv.at[2 + z], device_id={"lat": t}, device_id_type=MESH,
        )

    def reduced(t):
        return term(t, x, core) + recv1[t, x].astype(jnp.float32) + recv2[t].astype(jnp.float32)

    for t in range(nlat):
        @pl.when(z != t)
        def _():
            send3[t] = reduced(t).astype(send3.dtype)
            over_z(t).start()

    @pl.loop(0, rows)
    def _(i):
        for tile in range(tiles):
            source = jnp.concatenate(
                [
                    grads[i + q, pl.ds(tile * TILE, WINDOW), pl.ds(k * chs, chs)]
                    for q in range(SPAN)
                    for k in range(nbasis)
                ],
                axis=0,
            )
            made = jnp.dot(backward[i], source, preferred_element_type=jnp.float32)
            count = min(TILE, width - tile * TILE)
            grad_in[i, pl.ds(tile * TILE, count), :] = made[:count].astype(grad_in.dtype)

    grad_w[...] = reduced(z)
    for j in range(nlat):
        @pl.when(z != j)
        def _():
            pltpu.make_async_remote_copy(
                src_ref=send3.at[j], dst_ref=recv3.at[j], send_sem=g_send.at[2 + j],
                recv_sem=g_recv.at[2 + j], device_id={"lat": j}, device_id_type=MESH,
            ).wait_recv()
            grad_w[...] += recv3[j].astype(jnp.float32)
    grad_w[...] = grad_w[...] * factor

    for t in range(nlat):
        @pl.when(z != t)
        def _():
            over_z(t).wait_send()
    for t, kind, when in sends:
        @pl.when(when)
        def _():
            field_copy(t, kind).wait_send()
    for s in range(nshard):
        @pl.when(mine != s)
        def _():
            weight_copy(s).wait_send()
    for j in range(nlat):
        @pl.when(has_up & (j < z))
        def _():
            pass_on(j, 0).wait_send()
        @pl.when(has_down & (j > z))
        def _():
            pass_on(j, 1).wait_send()

    @pl.when(has_up)
    def _():
        cot_copy(0).wait_send()

    @pl.when(has_down)
    def _():
        cot_copy(1).wait_send()


def fused(features, basis, block_start, block_width, weight, cotangent):
    nlat, nchan, nlon = (lax.axis_size(a) for a in ("lat", "chan", "lon"))
    rows, width, chs = cotangent.shape
    part, depth = features.shape[2], weight.shape[0]
    factor = 1.0 / math.sqrt(rows * nlat * width * nchan * nlon)
    nbasis = basis.shape[1]
    table = basis.astype(jnp.float32).reshape(basis.shape[0], -1)
    field = ring_edges(jnp.swapaxes(features, 1, 2), 2, TILE)
    cot_ext = ring_edges(cotangent, 1, 16)
    ext, lanes = cot_ext.shape[1], field.shape[2]
    tiles = (width + TILE - 1) // TILE
    wide = max(ext, (tiles - 1) * TILE + WINDOW)
    tall, block = rows + 2 * REACH, depth // (nlat * nchan * nlon)
    half = jnp.bfloat16
    dma = pltpu.SemaphoreType.DMA
    smem = pl.BlockSpec(memory_space=pltpu.SMEM)
    vmem, anywhere = pl.BlockSpec(memory_space=pltpu.VMEM), pl.BlockSpec(memory_space=pl.ANY)
    return pl.pallas_call(
        functools.partial(layer_kernel, nlat, nchan, nlon, factor),
        out_shape=(
            jax.ShapeDtypeStruct((rows, width, chs), half),
            jax.ShapeDtypeStruct((rows, width, chs), half),
            jax.ShapeDtypeStruct((block, chs), jnp.float32),
        ),
        in_specs=[anywhere, anywhere, anywhere, vmem, smem, smem, smem],
        out_specs=(vmem, vmem, vmem),
        scratch_shapes=[
            pltpu.VMEM((rows, SPAN, 2 * TILE, nbasis * TILE), half),
            pltpu.VMEM((rows, TILE, SPAN * nbasis * WINDOW), half),
            pltpu.VMEM((tall, chs, lanes), half),
            pltpu.VMEM((tall, ext, chs), half),
            pltpu.VMEM((chs, depth), half),
            pltpu.VMEM((nchan * nlon, chs // (nchan * nlon), depth), half),
            pltpu.VMEM((rows, depth, tiles * TILE), half),
            pltpu.VMEM((tall, wide, depth), half),
            pltpu.VMEM((depth, chs), jnp.float32),
            pltpu.VMEM((nlat, nchan, block, chs), half),
            pltpu.VMEM((nlat, nchan, block, chs), half),
            pltpu.VMEM((nlat, block, chs), half),
            pltpu.VMEM((nlat, block, chs), half),
            pltpu.VMEM((nlat, block, chs), half),
            pltpu.VMEM((nlat, block, chs), half),
            dma((nlat, 3)),
            dma((nlat, 3)),
            dma((nlat, 2)),
            dma((nchan * nlon,)),
            dma((nchan * nlon,)),
            dma((2,)),
            dma((2,)),
            dma((5,)),
            dma((2 + nlat,)),
            dma((2 + nlat,)),
        ],
        compiler_params=pltpu.CompilerParams(
            collective_id=0, has_side_effects=True, vmem_limit_bytes=60 * 1024 * 1024
        ),
    )(field, cot_ext, weight.T, cotangent, table, block_start, block_width)


def on_device(features, basis, block_start, block_width, weight, cotangent):
    nlat, nchan, nlon = (lax.axis_size(a) for a in ("lat", "chan", "lon"))
    rows, _, chs = cotangent.shape
    shards = nchan * nlon
    tiled = chs % 128 == 0 and (chs // shards) % 16 == 0 and (chs // nlat) % 16 == 0 and (weight.shape[0] // (nlat * shards)) % 16 == 0
    if tiled and features.shape[2] * nlat == chs and nchan == 2 and nlon == 2 and nlat > 1 and rows >= REACH:
        run = fused
    else:
        run = plain
    return run(features, basis, block_start, block_width, weight, cotangent)


def solution(mesh):
    return jax.shard_map(
        on_device,
        mesh=mesh,
        in_specs=(
            P("group", ("chan", "lon"), "lat"),
            P(),
            P(),
            P(),
            P(None, ("chan", "lon")),
            P(("group", "lat"), ("chan", "lon"), None),
        ),
        out_specs=(
            P(("group", "lat"), ("chan", "lon"), None),
            P(("group", "lat"), ("chan", "lon"), None),
            P(("group", "lat", "chan", "lon"), None),
        ),
        check_vma=False,
    )
```

```python
import functools
import math

import jax
import jax.numpy as jnp
from jax import lax
from jax.experimental import pallas as pl
from jax.experimental.pallas import tpu as pltpu
from jax.sharding import PartitionSpec as P

REACH = 2


def padded(array, sides, width):
    for axis, dim in sides:
        size, length = (lax.axis_size(axis), array.shape[dim])
        up = [(i, (i + 1) % size) for i in range(size)]
        down = [(j, i) for i, j in up]
        last = lax.slice_in_dim(array, length - width, length, axis=dim)
        initial = lax.slice_in_dim(array, 0, width, axis=dim)
        before = lax.ppermute(last, axis, up)
        after = lax.ppermute(initial, axis, down)
        array = jnp.concatenate([before, array, after], axis=dim)
    return array


def extend(field, first, total_rows):
    haloed = padded(field, (("lat", 0), (("chan", "lon"), 1)), REACH)
    position = first - REACH + jnp.arange(haloed.shape[0], dtype=jnp.int32)
    inside = (position >= 0) & (position < total_rows)
    return jnp.where(inside[:, None, None], haloed, jnp.zeros_like(haloed))


def plain(features, basis, block_start, block_width, weight, cotangent):
    local = lax.all_to_all(features, "lat", split_axis=0, concat_axis=2, tiled=True)
    rows, width, chans = local.shape
    nbasis = basis.shape[1]
    span = 2 * REACH + 1
    total_rows = rows * lax.axis_size("lat")
    first = lax.axis_index("lat") * rows
    column = jnp.arange(span, dtype=jnp.int32)
    valid = (column[None, :] >= block_start[:, None]) & (
        column[None, :] < (block_start + block_width)[:, None]
    )
    blocks = jnp.where(valid[:, None, None, :], basis, jnp.zeros_like(basis))
    padded_blocks = jnp.pad(blocks, ((REACH, REACH), (0, 0), (0, 0), (0, 0)))
    near_blocks = lax.dynamic_slice_in_dim(padded_blocks, first, rows + 2 * REACH, 0).astype(
        jnp.float32
    )
    own_blocks = near_blocks[REACH : REACH + rows]
    reach_cols = width + 2 * REACH
    shift_table = (
        jnp.arange(reach_cols, dtype=jnp.int32)[None, :, None]
        - jnp.arange(width, dtype=jnp.int32)[:, None, None]
        == column[None, None, :]
    ).astype(jnp.float32)
    back_table = shift_table[:, :, ::-1]
    haloed = extend(local, first, total_rows)
    feat_parts = []
    for basis_k in range(nbasis):
        running = jnp.zeros((rows, width, chans), jnp.float32)
        for offset in range(span):
            row_map = jnp.einsum(
                "lmb,ib->ilm", shift_table, own_blocks[:, basis_k, offset, :]
            ).astype(jnp.bfloat16)
            running = running + jnp.einsum(
                "ilm,imc->ilc",
                row_map,
                haloed[offset : offset + rows],
                preferred_element_type=jnp.float32,
            )
        feat_parts.append(running.astype(jnp.bfloat16))
    feats = jnp.concatenate(feat_parts, axis=2)
    mixed = jnp.einsum(
        "ilj,jo->ilo",
        feats,
        lax.all_gather(weight, ("chan", "lon"), axis=1, tiled=True),
        preferred_element_type=jnp.float32,
    )
    grad_feats = jnp.einsum(
        "ilo,jo->ilj",
        cotangent,
        lax.all_gather(weight, ("chan", "lon"), axis=1, tiled=True),
        preferred_element_type=jnp.float32,
    )
    output = mixed.astype(jnp.bfloat16)
    factor = 1.0 / math.sqrt(total_rows * width * lax.axis_size(("chan", "lon")))
    grad_weight = lax.psum_scatter(
        lax.dot_general(
            feats, cotangent, (((0, 1), (0, 1)), ((), ())), preferred_element_type=jnp.float32
        )
        * factor,
        ("lat", "chan", "lon"),
        scatter_dimension=0,
        tiled=True,
    )
    grad_feats = grad_feats.astype(jnp.bfloat16)
    grad_halo = extend(grad_feats, first, total_rows)
    result = jnp.zeros((rows, width, chans), jnp.float32)
    for offset in range(span):
        begin = 2 * REACH - offset
        source_rows = grad_halo[begin : begin + rows]
        block_rows = near_blocks[begin : begin + rows]
        for basis_k in range(nbasis):
            back_map = jnp.einsum(
                "nmb,jb->jnm", back_table, block_rows[:, basis_k, offset, :]
            ).astype(jnp.bfloat16)
            source_part = source_rows[:, :, basis_k * chans : (basis_k + 1) * chans]
            result = result + jnp.einsum(
                "jnm,jmc->jnc", back_map, source_part, preferred_element_type=jnp.float32
            )
    grad_input = result.astype(jnp.bfloat16)
    return (output, grad_input, grad_weight)


SPAN = 2 * REACH + 1
TILE = 128
WINDOW = TILE + 16
MESH = pl.DeviceIdType.MESH


def ring_edges(array, dim, multiple):
    axes = ("chan", "lon")
    size, width = lax.axis_size(axes), array.shape[dim]
    up = [(i, (i + 1) % size) for i in range(size)]
    final = lax.slice_in_dim(array, width - REACH, width, axis=dim)
    initial = lax.slice_in_dim(array, 0, REACH, axis=dim)
    before = lax.ppermute(final, axes, up)
    after = lax.ppermute(initial, axes, [(j, i) for i, j in up])
    shape = list(array.shape)
    shape[dim] = -(width + 2 * REACH) % multiple
    return jnp.concatenate([before, array, after, jnp.zeros(shape, array.dtype)], axis=dim)


def layer_kernel(
    nlat, nchan, nlon, factor,
    field, cot_ext, weight_t, cot, basis, start, count_used,
    out, grad_in, grad_w,
    forward, backward, backward_far, padded_cot, held, landed, cots, mixing, gathered, feats, grads, total,
    send1, recv1, send2, recv2, send3, recv3,
    f_send, f_recv, fwd_send, w_send, w_recv, c_send, c_recv, own_sem, g_send, g_recv,
):
    z, x, core = lax.axis_index("lat"), lax.axis_index("chan"), lax.axis_index("lon")
    rows, width, chs = cot.shape
    ext, part, lanes = cot_ext.shape[1], field.shape[1], field.shape[2]
    wide = grads.shape[1]
    tiles = (width + TILE - 1) // TILE
    lanes_out = tiles * TILE
    nshard = nchan * nlon
    mine = x * nlon + core
    block = grad_w.shape[0]
    last = rows + REACH

    barrier = pltpu.get_barrier_semaphore()
    for t in range(nlat):
        @pl.when(z != t)
        def _():
            pl.semaphore_signal(barrier, inc=1, device_id={"lat": t}, device_id_type=MESH)
    for s in range(nshard):
        @pl.when(mine != s)
        def _():
            pl.semaphore_signal(
                barrier, inc=1, device_id={"chan": s // nlon, "lon": s % nlon}, device_id_type=MESH
            )
    pl.semaphore_wait(barrier, nlat - 1 + nshard - 1)

    def channels(j):
        return pl.ds(pl.multiple_of(j * part, 16), part)

    def piece(t, kind):
        if kind == 0:
            return rows * t, REACH, rows
        if kind == 1:
            return rows * t - REACH, 0, REACH
        return rows * (t + 1), last, REACH

    def field_copy(t, kind):
        begin, at, count = piece(t, kind)
        return pltpu.make_async_remote_copy(
            src_ref=field.at[pl.ds(begin, count)],
            dst_ref=landed.at[pl.ds(at, count), channels(z), :],
            send_sem=f_send.at[t, kind],
            recv_sem=f_recv.at[z, kind],
            device_id={"lat": t},
            device_id_type=MESH,
        )

    def arrival(j, kind):
        _, at, count = piece(1, kind)
        return pltpu.make_async_remote_copy(
            src_ref=field.at[pl.ds(0, count)],
            dst_ref=landed.at[pl.ds(at, count), channels(j), :],
            send_sem=f_send.at[0, kind],
            recv_sem=f_recv.at[j, kind],
            device_id={"lat": 0},
            device_id_type=MESH,
        )

    def direct(t, kind):
        if kind == 0:
            return z != t
        if kind == 1:
            return ((z > t) | (z == t - 1)) if t > 0 else None
        return ((z < t) | (z == t + 1)) if t < nlat - 1 else None

    kinds = ((t, kind) for kind in (0, 1, 2) for t in range(nlat))
    sends = [(t, kind, direct(t, kind)) for t, kind in kinds if direct(t, kind) is not None]
    for t, kind, when in sends:
        @pl.when(when)
        def _():
            field_copy(t, kind).start()

    def own_copy(t, kind):
        begin, at, count = piece(t, kind)
        return pltpu.make_async_copy(
            field.at[pl.ds(begin, count)], landed.at[pl.ds(at, count), channels(t), :], own_sem.at[kind]
        )

    for t, kind, _when in sends:
        @pl.when(z == t)
        def _():
            own_copy(t, kind).start()

    def weight_copy(s):
        return pltpu.make_async_remote_copy(
            src_ref=weight_t,
            dst_ref=gathered.at[mine],
            send_sem=w_send.at[s],
            recv_sem=w_recv.at[mine],
            device_id={"chan": s // nlon, "lon": s % nlon},
            device_id_type=MESH,
        )

    for s in range(nshard):
        @pl.when(mine != s)
        def _():
            weight_copy(s).start()
    own_weight = pltpu.make_async_copy(weight_t, gathered.at[mine], own_sem.at[3])
    own_weight.start()
    own_cot = pltpu.make_async_copy(cot_ext, cots.at[pl.ds(REACH, rows)], own_sem.at[4])
    own_cot.start()

    def cot_copy(way):
        begin, at = ((rows - REACH, 0), (0, last))[way]
        return pltpu.make_async_remote_copy(
            src_ref=cot_ext.at[pl.ds(begin, REACH)],
            dst_ref=cots.at[pl.ds(at, REACH)],
            send_sem=c_send.at[way],
            recv_sem=c_recv.at[way],
            device_id={"lat": lax.rem(z + 1 - 2 * way + nlat, nlat)},
            device_id_type=MESH,
        )

    has_up, has_down = z < nlat - 1, z > 0

    if wide > ext:
        grads[:, pl.ds(ext, wide - ext), :] = jnp.zeros(
            (rows + 2 * REACH, wide - ext, grads.shape[2]), grads.dtype
        )

    @pl.when(jnp.logical_not(has_down))
    def _():
        cots[pl.ds(0, REACH)] = jnp.zeros((REACH, ext, chs), cots.dtype)
        landed[pl.ds(0, REACH)] = jnp.zeros((REACH, chs, lanes), landed.dtype)

    @pl.when(jnp.logical_not(has_up))
    def _():
        cots[pl.ds(last, REACH)] = jnp.zeros((REACH, ext, chs), cots.dtype)
        landed[pl.ds(last, REACH)] = jnp.zeros((REACH, chs, lanes), landed.dtype)

    shift = lax.broadcasted_iota(jnp.int32, (TILE, WINDOW), 1) - lax.broadcasted_iota(
        jnp.int32, (TILE, WINDOW), 0
    )
    total_rows = rows * nlat
    nbasis = basis.shape[1] // (SPAN * SPAN)

    def value(row, k, a, b):
        held = jnp.clip(row, 0, total_rows - 1)
        used = (b >= start[held]) & (b < start[held] + count_used[held])
        used = used & (row >= 0) & (row < total_rows)
        return jnp.where(used, basis[held, (k * SPAN + a) * SPAN + b], 0.0)

    turned = lax.broadcasted_iota(jnp.int32, (2 * TILE, TILE), 0) - lax.broadcasted_iota(
        jnp.int32, (2 * TILE, TILE), 1
    )

    def band(row, k, a, back):
        offset = shift if back else turned
        made = jnp.zeros(offset.shape, jnp.float32)
        for b in range(SPAN):
            made = jnp.where(offset == (SPAN - 1 - b if back else b), value(row, k, a, b), made)
        return made

    @pl.loop(0, rows)
    def _(i):
        row = z * rows + i
        for k in range(nbasis):
            for a in range(SPAN):
                forward[i, pl.ds(a * 2 * TILE, 2 * TILE), pl.ds(k * TILE, TILE)] = band(
                    row, k, a, False
                ).astype(forward.dtype)

    def sources(i, here):
        return [q for q in range(SPAN) if (REACH <= i + q < last) == here]

    for i in range(rows):
        for here, maps in ((True, backward), (False, backward_far)):
            made = jnp.concatenate(
                [
                    band(z * rows + i + q - REACH, k, SPAN - 1 - q, True)
                    for q in sources(i, here)
                    for k in range(nbasis)
                ],
                axis=1,
            )
            maps[i, :, pl.ds(0, made.shape[1])] = made.astype(maps.dtype)

    for i in range(rows):
        padded_cot[pl.ds(i * lanes_out, width), :] = cot[i]
        if lanes_out > width:
            padded_cot[pl.ds(i * lanes_out + width, lanes_out - width), :] = jnp.zeros(
                (lanes_out - width, chs), padded_cot.dtype
            )

    own_weight.wait()
    for s in range(nshard):
        @pl.when(mine != s)
        def _():
            pltpu.make_async_remote_copy(
                src_ref=weight_t, dst_ref=gathered.at[s], send_sem=w_send.at[s],
                recv_sem=w_recv.at[s], device_id={"chan": s // nlon, "lon": s % nlon},
                device_id_type=MESH,
            ).wait_recv()
    mixing[...] = gathered[...].reshape(mixing.shape)

    def feature_gradient(q):
        grads[q, pl.ds(0, ext), :] = jnp.dot(
            cots[q], mixing[...], preferred_element_type=jnp.float32
        ).astype(grads.dtype)

    own_cot.wait()

    @pl.loop(REACH, last)
    def _(q):
        feature_gradient(q)

    def back_part(i, tile, here, maps):
        source = jnp.concatenate(
            [
                grads[i + q, pl.ds(tile * TILE, WINDOW), pl.ds(k * chs, chs)]
                for q in sources(i, here)
                for k in range(nbasis)
            ],
            axis=0,
        )
        return jnp.dot(
            maps[i, :, pl.ds(0, source.shape[0])], source, preferred_element_type=jnp.float32
        )

    for i in range(rows):
        for tile in range(tiles):
            held[i, pl.ds(tile * TILE, TILE), :] = back_part(i, tile, True, backward)

    def pass_on(j, way):
        begin, at, kind = ((last - REACH, 0, 1), (REACH, last, 2))[way]
        return pltpu.make_async_remote_copy(
            src_ref=landed.at[pl.ds(begin, REACH), channels(j), :],
            dst_ref=landed.at[pl.ds(at, REACH), channels(j), :],
            send_sem=fwd_send.at[j, way],
            recv_sem=f_recv.at[j, kind],
            device_id={"lat": z + 1 - 2 * way},
            device_id_type=MESH,
        )

    for t, kind, _when in sends:
        @pl.when(z == t)
        def _():
            own_copy(t, kind).wait()
    for j in range(nlat):
        @pl.when(z != j)
        def _():
            arrival(j, 0).wait_recv()
        @pl.when(has_up & (j < z))
        def _():
            pass_on(j, 0).start()
        @pl.when(has_down & (j > z))
        def _():
            pass_on(j, 1).start()
    @pl.when(has_up)
    def _():
        cot_copy(0).start()

    @pl.when(has_down)
    def _():
        cot_copy(1).start()

    for j in range(nlat):
        @pl.when((z != j) & has_down)
        def _():
            arrival(j, 1).wait_recv()
        @pl.when((z != j) & has_up)
        def _():
            arrival(j, 2).wait_recv()


    @pl.loop(0, rows)
    def _(i):
        for tile in range(tiles):
            reach = min(2 * TILE, lanes - tile * TILE)
            source = jnp.concatenate(
                [landed[i + a, :, pl.ds(tile * TILE, reach)] for a in range(SPAN)], axis=1
            )
            maps = jnp.concatenate(
                [forward[i, pl.ds(a * 2 * TILE, reach), :] for a in range(SPAN)], axis=0
            )
            made = jnp.dot(source, maps, preferred_element_type=jnp.float32)
            at = pl.ds(pl.multiple_of(i * lanes_out + tile * TILE, TILE), TILE)
            for k in range(nbasis):
                feats[pl.ds(k * chs, chs), at] = made[:, k * TILE : (k + 1) * TILE].astype(
                    feats.dtype
                )

    @pl.loop(0, total.shape[0] // TILE)
    def _(n):
        at = pl.ds(pl.multiple_of(n * TILE, TILE), TILE)
        total[at, :] = jnp.dot(
            feats[at, :], padded_cot[...], preferred_element_type=jnp.float32
        )

    def term(l, c, o):
        at = ((l * nchan + c) * nlon + o) * block
        return total[pl.ds(pl.multiple_of(at, 16), block), :]

    def exchange(send, recv, n, device):
        return pltpu.make_async_remote_copy(
            src_ref=send, dst_ref=recv, send_sem=g_send.at[n], recv_sem=g_recv.at[n],
            device_id=device, device_id_type=MESH,
        )

    for l in range(nlat):
        for c in range(nchan):
            send1[l, c] = term(l, c, 1 - core).astype(send1.dtype)
    over_core = exchange(send1, recv1, 0, {"lon": 1 - core})
    over_core.start()

    @pl.loop(0, rows)
    def _(i):
        at = pl.ds(pl.multiple_of(i * lanes_out, TILE), lanes_out)
        mixed = jnp.dot(mixing[...], feats[:, at], preferred_element_type=jnp.float32)
        out[i] = mixed.T[:width].astype(out.dtype)

    over_core.wait()

    for l in range(nlat):
        value = term(l, 1 - x, core) + recv1[l, 1 - x].astype(jnp.float32)
        send2[l] = value.astype(send2.dtype)
    over_x = exchange(send2, recv2, 1, {"chan": 1 - x})
    over_x.start()

    over_x.wait()

    def over_z(t):
        return pltpu.make_async_remote_copy(
            src_ref=send3.at[t], dst_ref=recv3.at[z], send_sem=g_send.at[2 + t],
            recv_sem=g_recv.at[2 + z], device_id={"lat": t}, device_id_type=MESH,
        )

    def reduced(t):
        return term(t, x, core) + recv1[t, x].astype(jnp.float32) + recv2[t].astype(jnp.float32)

    for t in range(nlat):
        @pl.when(z != t)
        def _():
            send3[t] = reduced(t).astype(send3.dtype)
            over_z(t).start()

    @pl.when(has_down)
    def _():
        cot_copy(0).wait_recv()

    @pl.when(has_up)
    def _():
        cot_copy(1).wait_recv()

    for q in (0, 1, last, last + 1):
        feature_gradient(q)
    for i in range(rows):
        for tile in range(tiles):
            made = held[i, pl.ds(tile * TILE, TILE), :]
            if sources(i, False):
                made = made + back_part(i, tile, False, backward_far)
            count = min(TILE, width - tile * TILE)
            grad_in[i, pl.ds(tile * TILE, count), :] = made[:count].astype(grad_in.dtype)

    grad_w[...] = reduced(z)
    for j in range(nlat):
        @pl.when(z != j)
        def _():
            pltpu.make_async_remote_copy(
                src_ref=send3.at[j], dst_ref=recv3.at[j], send_sem=g_send.at[2 + j],
                recv_sem=g_recv.at[2 + j], device_id={"lat": j}, device_id_type=MESH,
            ).wait_recv()
            grad_w[...] += recv3[j].astype(jnp.float32)
    grad_w[...] = grad_w[...] * factor

    for t in range(nlat):
        @pl.when(z != t)
        def _():
            over_z(t).wait_send()
    for t, kind, when in sends:
        @pl.when(when)
        def _():
            field_copy(t, kind).wait_send()
    for s in range(nshard):
        @pl.when(mine != s)
        def _():
            weight_copy(s).wait_send()
    for j in range(nlat):
        @pl.when(has_up & (j < z))
        def _():
            pass_on(j, 0).wait_send()
        @pl.when(has_down & (j > z))
        def _():
            pass_on(j, 1).wait_send()

    @pl.when(has_up)
    def _():
        cot_copy(0).wait_send()

    @pl.when(has_down)
    def _():
        cot_copy(1).wait_send()


def fused(features, basis, block_start, block_width, weight, cotangent):
    nlat, nchan, nlon = (lax.axis_size(a) for a in ("lat", "chan", "lon"))
    rows, width, chs = cotangent.shape
    part, depth = features.shape[2], weight.shape[0]
    factor = 1.0 / math.sqrt(rows * nlat * width * nchan * nlon)
    nbasis = basis.shape[1]
    table = basis.astype(jnp.float32).reshape(basis.shape[0], -1)
    field = ring_edges(jnp.swapaxes(features, 1, 2), 2, TILE)
    cot_ext = ring_edges(cotangent, 1, 16)
    ext, lanes = cot_ext.shape[1], field.shape[2]
    tiles = (width + TILE - 1) // TILE
    wide = max(ext, (tiles - 1) * TILE + WINDOW)
    tall, block = rows + 2 * REACH, depth // (nlat * nchan * nlon)
    half = jnp.bfloat16
    dma = pltpu.SemaphoreType.DMA
    smem = pl.BlockSpec(memory_space=pltpu.SMEM)
    vmem, anywhere = pl.BlockSpec(memory_space=pltpu.VMEM), pl.BlockSpec(memory_space=pl.ANY)
    return pl.pallas_call(
        functools.partial(layer_kernel, nlat, nchan, nlon, factor),
        out_shape=(
            jax.ShapeDtypeStruct((rows, width, chs), half),
            jax.ShapeDtypeStruct((rows, width, chs), half),
            jax.ShapeDtypeStruct((block, chs), jnp.float32),
        ),
        in_specs=[anywhere, anywhere, anywhere, vmem, smem, smem, smem],
        out_specs=(vmem, vmem, vmem),
        scratch_shapes=[
            pltpu.VMEM((rows, SPAN * 2 * TILE, nbasis * TILE), half),
            pltpu.VMEM((rows, TILE, SPAN * nbasis * WINDOW), half),
            pltpu.VMEM((rows, TILE, SPAN * nbasis * WINDOW), half),
            pltpu.VMEM((rows * tiles * TILE, chs), half),
            pltpu.VMEM((rows, tiles * TILE, chs), jnp.float32),
            pltpu.VMEM((tall, chs, lanes), half),
            pltpu.VMEM((tall, ext, chs), half),
            pltpu.VMEM((chs, depth), half),
            pltpu.VMEM((nchan * nlon, chs // (nchan * nlon), depth), half),
            pltpu.VMEM((depth, rows * tiles * TILE), half),
            pltpu.VMEM((tall, wide, depth), half),
            pltpu.VMEM((depth, chs), jnp.float32),
            pltpu.VMEM((nlat, nchan, block, chs), half),
            pltpu.VMEM((nlat, nchan, block, chs), half),
            pltpu.VMEM((nlat, block, chs), half),
            pltpu.VMEM((nlat, block, chs), half),
            pltpu.VMEM((nlat, block, chs), half),
            pltpu.VMEM((nlat, block, chs), half),
            dma((nlat, 3)),
            dma((nlat, 3)),
            dma((nlat, 2)),
            dma((nchan * nlon,)),
            dma((nchan * nlon,)),
            dma((2,)),
            dma((2,)),
            dma((5,)),
            dma((2 + nlat,)),
            dma((2 + nlat,)),
        ],
        compiler_params=pltpu.CompilerParams(
            collective_id=0, has_side_effects=True, vmem_limit_bytes=60 * 1024 * 1024
        ),
    )(field, cot_ext, weight.T, cotangent, table, block_start, block_width)


def on_device(features, basis, block_start, block_width, weight, cotangent):
    nlat, nchan, nlon = (lax.axis_size(a) for a in ("lat", "chan", "lon"))
    rows, _, chs = cotangent.shape
    shards = nchan * nlon
    tiled = chs % 128 == 0 and weight.shape[0] % TILE == 0 and (chs // shards) % 16 == 0 and (chs // nlat) % 16 == 0 and (weight.shape[0] // (nlat * shards)) % 16 == 0
    if tiled and features.shape[2] * nlat == chs and nchan == 2 and nlon == 2 and nlat > 1 and rows >= REACH:
        run = fused
    else:
        run = plain
    return run(features, basis, block_start, block_width, weight, cotangent)


def solution(mesh):
    return jax.shard_map(
        on_device,
        mesh=mesh,
        in_specs=(
            P("group", ("chan", "lon"), "lat"),
            P(),
            P(),
            P(),
            P(None, ("chan", "lon")),
            P(("group", "lat"), ("chan", "lon"), None),
        ),
        out_specs=(
            P(("group", "lat"), ("chan", "lon"), None),
            P(("group", "lat"), ("chan", "lon"), None),
            P(("group", "lat", "chan", "lon"), None),
        ),
        check_vma=False,
    )
```
